128 devices in a mesh: gx: 16 (over y, z_hi, core), gy: 8 (over z_lo, x).
Axes of the slice: x: 4, y: 4, z: 4 (z_hi: 2, z_lo: 2; z = z_hi * 2 + z_lo), core: 2. Of those that a mesh axis runs over, the one named last changes fastest.
Arguments:
- tokens: bfloat16 [1024, 16384], P(('gx', 'gy')), may hold values from -6 to 6
- queries: bfloat16 [1024, 16384], P(('gx', 'gy')), may hold values from -240 to 240
- page_pool: bfloat16 [4096, 2, 16, 1024], P(('gx', 'gy')), may hold values from -6 to 6
- new_pages: bfloat16 [2048, 2, 16, 1024], P(('gx', 'gy')), may hold values from -6 to 6
- page_table: int32 [2048, 2], P(('gx', 'gy')), may hold values from 0 to 15, as said below
- block_table: int32 [1024, 8], P(('gx', 'gy')), may hold values from 0 to 63, as said below
- context: int32 [1024], P(('gx', 'gy')), may hold values from 1 to 128, as said below
- norm_gain: float32 [16384], replicated, may hold values from 0.1 to 1.9
- gate_weight: bfloat16 [16384, 26624], P('gy', 'gx'), may hold values from -0.046875 to 0.046875
- up_weight: bfloat16 [16384, 26624], P('gy', 'gx'), may hold values from -0.046875 to 0.046875
- down_weight: bfloat16 [26624, 16384], P('gx', 'gy'), may hold values from -0.0390625 to 0.0390625
Outputs:
- layer_out: bfloat16 [1024, 16384], P('gx', 'gy')
The draws below stay inside these ranges and needn't reach their ends.
Inputs may be any that keep to these rules, and one draw needn't show every extreme that they name: `page_table`: column 0 is an owner index along gx, column 1 a slot below 2; the new pages of one device name distinct (owner, slot) pairs, and each device fills all 2 slots of some owner. `block_table`: an entry below 32 names a resident page; 32 + s * 2 + r names the page that the device with gx index s placed at slot r; only filled slots are named. `context`: every device has a row of length 128.
All inputs are finite; a program needn't handle non-finite values.
Results may differ from the reference program's by a relative error of at most 0.006.
Values may be sent and summed in bfloat16 or wider, within the bound.
No kernel may reach another device: no remote copies, remote signals or barrier semaphores. Data moves between devices by JAX's collectives and lax.ppermute only.
A program may use at most 128 MiB of HBM per device.

```python
import jax
import jax.numpy as jnp
from jax import lax

D = 16384
HQ = 128
HD = 128
KVH = 8
FF = 26624
ROWS_DEV = 8
PAGE = 16
MAXB = 8
POOL = 32
CAP = 2
NEWP = 16
TOKENS = 1024
N_GX = 16
N_GY = 8
DEVICES = 128


def plan_pages(key):
    key = jax.random.fold_in(key, 11)
    area_size = N_GX * CAP

    def one_source(source_key):
        pick_key, order_key, shuffle_key = jax.random.split(source_key, 3)
        full_owner = jax.random.randint(pick_key, (), 0, N_GX)
        ranking = jax.random.permutation(order_key, area_size)
        slot_index = jnp.arange(area_size, dtype=jnp.int32)
        priority = jnp.where(slot_index // CAP == full_owner, slot_index - area_size, ranking)
        chosen = jnp.argsort(priority, stable=True)[:NEWP]
        return chosen[jax.random.permutation(shuffle_key, NEWP)].astype(jnp.int32)
    chosen = jax.vmap(one_source)(jax.random.split(key, N_GX * N_GY))
    return chosen.reshape(-1)


def draw_page_table(key, part):
    chosen = plan_pages(key)
    return jnp.stack([chosen // CAP, chosen % CAP], axis=1).astype(jnp.int32)


def draw_block_table(key, part):
    chosen = plan_pages(key)
    key = jax.random.fold_in(key, 5)
    device_count = N_GX * N_GY
    area_size = N_GX * CAP
    store_size = POOL + area_size
    source = jnp.arange(device_count * NEWP, dtype=jnp.int32) // NEWP
    target = (chosen // CAP * N_GY + source % N_GY) * area_size + source // N_GY * CAP + chosen % CAP
    filled = jnp.zeros((device_count * area_size,), jnp.int32).at[target].set(1).reshape(device_count, area_size)
    valid = jnp.concatenate([jnp.ones((device_count, POOL), jnp.int32), filled], axis=1)

    def one_device(device_key, valid_row):
        order_key, pick_key = jax.random.split(device_key)
        ranking = jax.random.permutation(order_key, store_size)
        order = jnp.argsort((1 - valid_row) * store_size + ranking, stable=True).astype(jnp.int32)
        count = jnp.sum(valid_row)
        picks = jax.random.randint(pick_key, (ROWS_DEV, MAXB), 0, count)
        return order[picks]
    tables = jax.vmap(one_device)(jax.random.split(key, device_count), valid)
    return tables.reshape(TOKENS, MAXB).astype(jnp.int32)


def draw_context(key, part):
    key = jax.random.fold_in(key, 7)
    length_key, row_key = jax.random.split(key)
    device_count = N_GX * N_GY
    lengths = jax.random.randint(length_key, (device_count, ROWS_DEV), 1, MAXB * PAGE + 1)
    full_row = jax.random.randint(row_key, (device_count, 1), 0, ROWS_DEV)
    lengths = jnp.where(jnp.arange(ROWS_DEV, dtype=jnp.int32)[None, :] == full_row, MAXB * PAGE, lengths)
    return lengths.reshape(TOKENS).astype(jnp.int32)


def draw_queries(key, part):
    key = jax.random.fold_in(key, 3)
    value_key = jax.random.fold_in(key, 0)
    values = jnp.clip(jax.random.normal(value_key, (TOKENS, HQ, HD), jnp.float32), -6.0, 6.0)
    return values.reshape(TOKENS, HQ * HD).astype(jnp.bfloat16)


def levels(own_key, extent, cuts, low, largest):
    factor_of = 1.0
    for dim, shards_of in cuts:
        heights = jax.random.uniform(jax.random.fold_in(jax.random.fold_in(own_key, 6), dim), (shards_of,), jnp.float32, low / len(cuts), largest / len(cuts))
        factor_of = factor_of * jnp.repeat(jnp.exp(heights), extent[dim] // shards_of).reshape((-1,) + (1,) * (len(extent) - 1 - dim))
    return factor_of


def scatter_about(stream_key, extent, width, reach, cuts=(), kind=jnp.bfloat16):
    entries = jax.random.normal(stream_key, extent, jnp.float32) * width
    if len(cuts) > 0:
        entries = levels(stream_key, extent, cuts, -0.22, 0.18) * entries
    return jnp.clip(entries, min=-reach, max=reach).astype(kind)


def setup_inputs(seed: int = 0) -> dict:
    streams_of = jax.random.split(jax.random.key(seed), 12)
    return {
        "tokens": scatter_about(streams_of[0], (TOKENS, D), 1.0, 6.0, ((0, 128),)),
        "queries": draw_queries(jax.random.fold_in(streams_of[11], 71), 0),
        "page_pool": scatter_about(streams_of[2], (DEVICES * POOL, 2, PAGE, KVH * HD), 1.0, 6.0, ((0, 128),)),
        "new_pages": scatter_about(streams_of[3], (DEVICES * NEWP, 2, PAGE, KVH * HD), 1.0, 6.0, ((0, 128),)),
        "page_table": draw_page_table(jax.random.fold_in(streams_of[11], 71), 0),
        "block_table": draw_block_table(jax.random.fold_in(streams_of[11], 71), 0),
        "context": draw_context(jax.random.fold_in(streams_of[11], 71), 0),
        "norm_gain": jnp.clip(1.0 + 0.18 * jax.random.normal(streams_of[7], (D,), jnp.float32), 0.1, 1.9),
        "gate_weight": scatter_about(streams_of[8], (D, FF), D ** -0.5, 0.046875, ((0, 8), (1, 16))),
        "up_weight": scatter_about(streams_of[9], (D, FF), D ** -0.5, 0.046875, ((0, 8), (1, 16))),
        "down_weight": scatter_about(streams_of[10], (FF, D), FF ** -0.5, 0.0390625, ((0, 16), (1, 8))),
    }


def attend_device(operands):
    page_store, query_rows, table_rows, length_rows = operands
    row_count = query_rows.shape[0]
    key_span = MAXB * PAGE
    picked = page_store[table_rows]
    page_keys = picked[:, :, 0].reshape(row_count, key_span, KVH, HD).astype(jnp.float32)
    page_values = picked[:, :, 1].reshape(row_count, key_span, KVH, HD).astype(jnp.float32)
    grouped = query_rows.reshape(row_count, KVH, HQ // KVH, HD).astype(jnp.float32)
    scores = jnp.einsum('rkgd,rlkd->rkgl', grouped, page_keys) * (1.0 / HD ** 0.5)
    visible = jnp.arange(key_span, dtype=jnp.int32)[None, :] < length_rows[:, None]
    scores = jnp.where(visible[:, None, None, :], scores, jnp.float32(-1e+30))
    probs = jax.nn.softmax(scores, axis=-1).astype(jnp.bfloat16).astype(jnp.float32)
    attended = jnp.einsum('rkgl,rlkd->rkgd', probs, page_values)
    return attended.reshape(row_count, HQ * HD)

def reference(tokens, queries, page_pool, new_pages, page_table, block_table, context, norm_gain, gate_weight, up_weight, down_weight):
    device_count = N_GX * N_GY
    area_size = N_GX * CAP
    source = jnp.arange(device_count * NEWP, dtype=jnp.int32) // NEWP
    source_gx = source // N_GY
    source_gy = source % N_GY
    target = (page_table[:, 0] * N_GY + source_gy) * area_size + source_gx * CAP + page_table[:, 1]
    page_shape = new_pages.shape[1:]
    arrivals = jnp.zeros((device_count * area_size,) + page_shape, jnp.bfloat16).at[target].set(new_pages)
    page_store = jnp.concatenate([page_pool.reshape((device_count, POOL) + page_shape), arrivals.reshape((device_count, area_size) + page_shape)], axis=1)
    attended = lax.map(attend_device, (page_store, queries.reshape(device_count, ROWS_DEV, D), block_table.reshape(device_count, ROWS_DEV, MAXB), context.reshape(device_count, ROWS_DEV)))
    attended = attended.reshape(TOKENS, D)
    mixed = (tokens.astype(jnp.float32) + attended).astype(jnp.bfloat16)
    mixed_wide = mixed.astype(jnp.float32)
    normed = (mixed_wide * lax.rsqrt(lax.optimization_barrier(jnp.mean(mixed_wide * mixed_wide, axis=-1, keepdims=True)) + 1e-05) * norm_gain).astype(jnp.bfloat16)
    gate = jnp.dot(normed, gate_weight, preferred_element_type=jnp.float32)
    up_proj = jnp.dot(normed, up_weight, preferred_element_type=jnp.float32)
    hidden = (jax.nn.silu(gate) * up_proj).astype(jnp.bfloat16)
    return (mixed_wide + jnp.dot(hidden, down_weight, preferred_element_type=jnp.float32)).astype(jnp.bfloat16)
```

```python
import jax
import jax.numpy as jnp
from jax import lax
from jax.sharding import Mesh, PartitionSpec as P

HD = 128
KVH = 8
PAGE = 16
CAP = 2
GX = ("y", "zh", "c")
GY = ("zl", "x")
CHIPS = ("y", "zh")
SWAP = [(0, 1), (1, 0)]


def score_keys(grouped, page_keys):
    return jnp.einsum("rkgd,rlkd->rkgl", grouped, page_keys, preferred_element_type=jnp.float32) * (
        1.0 / HD**0.5
    )


def page_rows(page_store, table_rows, key_span):
    picked = page_store[table_rows]
    row_count = table_rows.shape[0]
    page_keys = picked[:, :, 0].reshape(row_count, key_span, KVH, HD)
    page_values = picked[:, :, 1].reshape(row_count, key_span, KVH, HD)
    return (page_keys, page_values)


def attend(tokens, queries, page_pool, new_pages, page_table, block_table, context):
    row_count, model_width = tokens.shape
    area_size = lax.axis_size(GX) * CAP
    send_slot = page_table[:, 0] * CAP + page_table[:, 1]
    holder = jnp.argmax(jnp.arange(area_size)[:, None] == send_slot[None, :], axis=1)
    arrived = lax.all_to_all(new_pages[holder], GX, split_axis=0, concat_axis=0, tiled=True)
    grouped = queries.reshape(row_count, KVH, model_width // (KVH * HD), HD)
    key_span = block_table.shape[1] * PAGE
    page_store = jnp.concatenate([page_pool, arrived], axis=0)
    page_keys, page_values = page_rows(page_store, block_table, key_span)
    scores = score_keys(grouped, page_keys)
    visible = jnp.arange(key_span, dtype=jnp.int32)[None, :] < context[:, None]
    scores = jnp.where(visible[:, None, None, :], scores, jnp.float32(-1e30))
    probs = jax.nn.softmax(scores, axis=-1).astype(jnp.bfloat16)
    attended = jnp.einsum(
        "rkgl,rlkd->rkgd", probs, page_values, preferred_element_type=jnp.float32
    ).reshape(row_count, model_width)
    return (tokens.astype(jnp.float32) + attended).astype(jnp.bfloat16)


def spread(mixed_rows, norm_gain):
    row_count, model_width = mixed_rows.shape
    parts = lax.axis_size(GY)
    width = model_width // parts
    mixed_wide = mixed_rows.astype(jnp.float32)
    scale = lax.rsqrt(jnp.mean(mixed_wide * mixed_wide, axis=-1, keepdims=True) + 1e-05)
    high = scale.astype(jnp.bfloat16)
    rest = scale - high.astype(jnp.float32)
    middle = rest.astype(jnp.bfloat16)
    low = (rest - middle.astype(jnp.float32)).astype(jnp.bfloat16)
    terms = jnp.concatenate([high, middle, low, jnp.zeros((row_count, 125), jnp.bfloat16)], axis=1)
    payload = jnp.concatenate(
        [
            mixed_rows.reshape(row_count, parts, width),
            jnp.broadcast_to(terms[:, None, :], (row_count, parts, 128)),
        ],
        axis=2,
    )
    block = lax.all_to_all(payload, GY, split_axis=1, concat_axis=0, tiled=True)
    block = block.reshape(row_count * parts, width + 128)
    resid = block[:, :width].astype(jnp.float32)
    scale = (
        block[:, width : width + 1].astype(jnp.float32)
        + block[:, width + 1 : width + 2].astype(jnp.float32)
        + block[:, width + 2 : width + 3].astype(jnp.float32)
    )
    gain = lax.dynamic_slice(norm_gain, (lax.axis_index(GY) * width,), (width,))
    return resid, (resid * scale * gain).astype(jnp.bfloat16)


def on_device(
    tokens,
    queries,
    page_pool,
    new_pages,
    page_table,
    block_table,
    context,
    norm_gain,
    gate_weight,
    up_weight,
    down_weight,
):
    mixed_rows = attend(tokens, queries, page_pool, new_pages, page_table, block_table, context)
    resid, normed_block = spread(mixed_rows, norm_gain)

    return feed_forward(resid, normed_block, gate_weight, up_weight, down_weight)


def dot(a, b):
    return jnp.dot(a, b, preferred_element_type=jnp.float32)


def wide(a):
    return a.astype(jnp.float32)


def narrow(a):
    return a.astype(jnp.bfloat16)


def swap(a, axis):
    return lax.ppermute(a, axis, [(0, 1), (1, 0)])


def halves(a, axis):
    rows = a.shape[0] // 2
    me = lax.axis_index(axis)
    mine = lax.dynamic_slice_in_dim(a, me * rows, rows, 0)
    theirs = lax.dynamic_slice_in_dim(a, (1 - me) * rows, rows, 0)
    return mine, theirs


def join(mine, axis):
    came = swap(mine, axis)
    first = lax.axis_index(axis) == 0
    return jnp.concatenate([jnp.where(first, mine, came), jnp.where(first, came, mine)], axis=0)


def x_sum(part):
    rows, width = part.shape
    came = lax.all_to_all(part.reshape(4, rows // 4, width), "x", split_axis=0, concat_axis=0, tiled=True)
    return jnp.sum(wide(came), axis=0)


def x_gather(a):
    rows, width = a.shape
    came = lax.all_to_all(
        jnp.broadcast_to(a[None], (4, rows, width)), "x", split_axis=0, concat_axis=0, tiled=True
    )
    return came.reshape(4 * rows, width)


def hidden_of(sums):
    width = sums.shape[1] // 2
    return narrow(jax.nn.silu(sums[:, :width]) * sums[:, width:])


def hidden_x_first(part):
    mine, theirs = halves(x_sum(part), "zl")
    sums = mine + wide(swap(narrow(theirs), "zl"))
    return x_gather(join(hidden_of(sums), "zl"))


def hidden_z_first(part):
    mine, theirs = halves(part, "zl")
    half = narrow(wide(mine) + wide(swap(theirs, "zl")))
    return join(x_gather(hidden_of(x_sum(half))), "zl")


def feed_forward(resid, normed_block, gate_weight, up_weight, down_weight):
    rows, width = normed_block.shape
    weight = jnp.concatenate([gate_weight, up_weight], axis=1)
    chip = jnp.concatenate([normed_block, swap(normed_block, "c")], axis=0)
    quad = jnp.concatenate([chip, swap(chip, "zh")], axis=0)
    total = jnp.zeros((2, rows, width), jnp.float32)
    for shift, hidden_from in ((0, hidden_x_first), (1, hidden_z_first), (3, hidden_x_first), (2, hidden_z_first)):
        piece = quad
        if shift:
            piece = lax.ppermute(quad, "y", [((i + shift) % 4, i) for i in range(4)])
        hidden = hidden_from(narrow(dot(piece, weight)))
        down = dot(hidden, down_weight).reshape(2, 2, rows, width)
        came = swap(narrow(down[:, 1]), "c")
        part = down[:, 0] + wide(came)
        if shift:
            part = wide(lax.ppermute(narrow(part), "y", [(i, (i + shift) % 4) for i in range(4)]))
        total = total + part
    ffn_block = total[0] + wide(swap(narrow(total[1]), "zh"))
    return narrow(resid + ffn_block)


def solution(mesh):
    fine = Mesh(mesh.devices.reshape(4, 2, 2, 2, 4), GX + GY)
    rows = P(GX + GY)
    return jax.shard_map(
        on_device,
        mesh=fine,
        in_specs=(rows,) * 7 + (P(), P(GY, GX), P(GY, GX), P(GX, GY)),
        out_specs=P(GX, GY),
        check_vma=False,
    )
```

```python
import functools

import jax
import jax.numpy as jnp
from jax import lax
from jax.experimental import pallas as pl
from jax.experimental.pallas import tpu as pltpu
from jax.sharding import Mesh, PartitionSpec as P

HD = 128
KVH = 8
PAGE = 16
CAP = 2
GX = ("y", "zh", "c")
GY = ("zl", "x")
CHIPS = ("y", "zh")
SWAP = [(0, 1), (1, 0)]


def attend_kernel(table, context, queries, pool, arrived, _, out, store, sems):
    row_count, blocks = table.shape
    resident = pool.shape[0]
    heads = queries.shape[1] // KVH
    span = blocks * PAGE

    @pl.loop(0, row_count)
    def _(t):
        for i in range(blocks):
            page = table[t, i]
            place = store.at[t, :, pl.ds(i * PAGE, PAGE)]

            @pl.when(page < resident)
            def _():
                pltpu.make_async_copy(pool.at[page], place, sems.at[t]).start()

            @pl.when(page >= resident)
            def _():
                pltpu.make_async_copy(arrived.at[page - resident], place, sems.at[t]).start()

    @pl.loop(0, row_count)
    def _(t):
        pltpu.make_async_copy(store.at[t], store.at[t], sems.at[t]).wait()
        scores = jnp.concatenate(
            [
                lax.dot_general(
                    queries[t, k * heads : (k + 1) * heads, :],
                    store[t, 0, :, k * HD : (k + 1) * HD],
                    (((1,), (1,)), ((), ())),
                    preferred_element_type=jnp.float32,
                )
                for k in range(KVH)
            ],
            axis=0,
        ) * (1.0 / HD**0.5)
        visible = lax.broadcasted_iota(jnp.int32, scores.shape, 1) < context[t]
        scores = jnp.where(visible, scores, jnp.float32(-1e30))
        weights = jnp.exp(scores - jnp.max(scores, axis=1, keepdims=True))
        probs = narrow(weights / jnp.sum(weights, axis=1, keepdims=True))
        for k in range(KVH):
            rows = slice(k * heads, (k + 1) * heads)
            out[t, rows, :] = dot(probs[rows], store[t, 1, :, k * HD : (k + 1) * HD])


def attend(tokens, queries, page_pool, new_pages, page_table, block_table, context, after):
    row_count, model_width = tokens.shape
    area_size = lax.axis_size(GX) * CAP
    send_slot = page_table[:, 0] * CAP + page_table[:, 1]
    holder = jnp.argmax(jnp.arange(area_size)[:, None] == send_slot[None, :], axis=1)
    arrived = lax.all_to_all(new_pages[holder], GX, split_axis=0, concat_axis=0, tiled=True)
    heads = model_width // HD
    span = block_table.shape[1] * PAGE
    smem, vmem, anywhere = (pl.BlockSpec(memory_space=m) for m in (pltpu.SMEM, pltpu.VMEM, pl.ANY))
    attended = pl.pallas_call(
        attend_kernel,
        name="attend",
        out_shape=jax.ShapeDtypeStruct((row_count, heads, HD), jnp.float32),
        in_specs=[smem, smem, vmem] + [anywhere] * 3,
        out_specs=vmem,
        scratch_shapes=[
            pltpu.VMEM((row_count, 2, span, KVH * HD), jnp.bfloat16),
            pltpu.SemaphoreType.DMA((row_count,)),
        ],
        cost_estimate=pl.CostEstimate(flops=2**27, bytes_accessed=2**23, transcendentals=2**17),
        compiler_params=pltpu.CompilerParams(vmem_limit_bytes=8 * 2**20),
    )(block_table, context, queries.reshape(row_count, heads, HD), page_pool, arrived, after)
    return narrow(wide(tokens) + attended.reshape(row_count, model_width))


def spread(mixed_rows, norm_gain):
    row_count, model_width = mixed_rows.shape
    parts = lax.axis_size(GY)
    width = model_width // parts
    mixed_wide = mixed_rows.astype(jnp.float32)
    scale = lax.rsqrt(jnp.mean(mixed_wide * mixed_wide, axis=-1, keepdims=True) + 1e-05)
    high = scale.astype(jnp.bfloat16)
    rest = scale - high.astype(jnp.float32)
    middle = rest.astype(jnp.bfloat16)
    low = (rest - middle.astype(jnp.float32)).astype(jnp.bfloat16)
    terms = jnp.concatenate([high, middle, low, jnp.zeros((row_count, 125), jnp.bfloat16)], axis=1)
    payload = jnp.concatenate(
        [
            mixed_rows.reshape(row_count, parts, width),
            jnp.broadcast_to(terms[:, None, :], (row_count, parts, 128)),
        ],
        axis=2,
    )
    block = lax.all_to_all(payload, GY, split_axis=1, concat_axis=0, tiled=True)
    block = block.reshape(row_count * parts, width + 128)
    resid = block[:, :width].astype(jnp.float32)
    scale = (
        block[:, width : width + 1].astype(jnp.float32)
        + block[:, width + 1 : width + 2].astype(jnp.float32)
        + block[:, width + 2 : width + 3].astype(jnp.float32)
    )
    gain = lax.dynamic_slice(norm_gain, (lax.axis_index(GY) * width,), (width,))
    return resid, (resid * scale * gain).astype(jnp.bfloat16)


def on_device(
    tokens,
    queries,
    page_pool,
    new_pages,
    page_table,
    block_table,
    context,
    norm_gain,
    gate_weight,
    up_weight,
    down_weight,
):
    gate_weight, up_weight, down_weight, mark = load(gate_weight, up_weight, down_weight)
    mixed_rows = attend(tokens, queries, page_pool, new_pages, page_table, block_table, context, mark)
    resid, normed_block = spread(mixed_rows, norm_gain)

    return feed_forward(resid, normed_block, gate_weight, up_weight, down_weight)


def dot(a, b):
    return jnp.dot(a, b, preferred_element_type=jnp.float32)


def wide(a):
    return a.astype(jnp.float32)


def narrow(a):
    return a.astype(jnp.bfloat16)


def swap(a, axis):
    return lax.ppermute(a, axis, [(0, 1), (1, 0)])


def send(a, axis, shift):
    return lax.ppermute(a, axis, [(i, (i + shift) % 4) for i in range(4)])


def call(kernel, name, outs, *operands, after=()):
    count = len(operands)
    vmem, anywhere = pl.BlockSpec(memory_space=pltpu.VMEM), pl.BlockSpec(memory_space=pl.ANY)
    return pl.pallas_call(
        lambda *refs: kernel(*refs[:count], *refs[count + len(after) :]),
        name=name,
        out_shape=[jax.ShapeDtypeStruct(shape, dtype) for shape, dtype in outs],
        in_specs=[vmem] * count + [anywhere] * len(after),
        out_specs=[vmem] * len(outs),
        cost_estimate=pl.CostEstimate(flops=2**34, bytes_accessed=1024, transcendentals=0),
        compiler_params=pltpu.CompilerParams(vmem_limit_bytes=8 * 2**20),
    )(*operands, *after)


def load_kernel(*refs):
    mark, sems = refs[-2:]
    count = len(refs) // 2 - 1
    mark[...] = jnp.zeros_like(mark)
    copies = [pltpu.make_async_copy(refs[i], refs[count + i], sems.at[i]) for i in range(count)]
    for copy in copies:
        copy.start()
    for copy in copies:
        copy.wait()


def load(*weights):
    return pl.pallas_call(
        load_kernel,
        name="load",
        out_shape=[pltpu.VMEM(w.shape, w.dtype) for w in weights] + [jax.ShapeDtypeStruct((8, 128), jnp.float32)],
        in_specs=[pl.BlockSpec(memory_space=pltpu.HBM)] * len(weights),
        out_specs=[pl.BlockSpec(memory_space=pltpu.VMEM)] * (len(weights) + 1),
        scratch_shapes=[pltpu.SemaphoreType.DMA((len(weights),))],
        cost_estimate=pl.CostEstimate(flops=0, bytes_accessed=2**25, transcendentals=0),
        compiler_params=pltpu.CompilerParams(vmem_limit_bytes=8 * 2**20),
    )(*weights)


def span(masks):
    names = [0]
    for mask in masks:
        names = names + [name ^ mask for name in names]
    return names


def exchange(a, mask):
    if mask == 4:
        return lax.ppermute(a, "zl", [(0, 1), (1, 0)])
    return lax.ppermute(a, "x", [(i, i ^ mask) for i in range(4)])


def up_kernel(masks, own, other, gate, up, keep, away):
    width = gate.shape[1]
    whole = width // 256 * 256
    kept = span(masks[1:])

    def put(columns, block):
        for h in range(2):
            for j in range(2):
                for d in range(4):
                    name, row = h * 4 + d, ((h * 2 + j) * 4 + d) * 16
                    out = keep if name in kept else away
                    place = kept.index(name if name in kept else name ^ masks[0]) * 32 + j * 16
                    out[place : place + 16, columns] = block[row : row + 16].astype(out.dtype)

    rows = jnp.concatenate([core[h * 64 : (h + 1) * 64, :] for h in range(2) for core in (own, other)], axis=0)

    @pl.loop(0, whole // 256)
    def _(i):
        start = pl.multiple_of(i * 256, 256)
        put(pl.ds(start, 256), dot(rows, gate[:, pl.ds(start, 256)]))
        put(pl.ds(pl.multiple_of(width + start, 128), 256), dot(rows, up[:, pl.ds(start, 256)]))

    last = dot(rows, jnp.concatenate([gate[:, whole:], up[:, whole:]], axis=1))
    put(pl.ds(whole, width - whole), last[:, : width - whole])
    put(pl.ds(width + whole, width - whole), last[:, width - whole :])


def add_kernel(masks, mine, came, keep, away):
    names, kept = span(masks), span(masks[1:])
    for out, flip in ((keep, 0), (away, masks[0])):
        for place, name in enumerate(kept):
            row = names.index(name ^ flip) * 32
            total = mine[row : row + 32, :] + wide(came[row : row + 32, :])
            out[place * 32 : (place + 1) * 32, :] = total.astype(out.dtype)


def hidden_kernel(mine, came, out):
    width = out.shape[1]

    def total(columns):
        return mine[:, columns] + wide(came[:, columns])

    gate = total(slice(0, width))
    out[...] = narrow(gate * (1.0 / (1.0 + jnp.exp(-gate))) * total(slice(width, 2 * width)))


def join_kernel(mine, came, out):
    rows = mine.shape[0]
    out[:rows, :] = mine[...]
    out[rows:, :] = came[...]


def down_kernel(masks, mine, came, weight, keep, away):
    names, rows = span(masks), []
    for h in range(2):
        for j in range(2):
            for d in range(4):
                half, place = divmod(names.index(h * 4 + d), 4)
                row = place * 32 + j * 16
                rows.append((mine, came)[half][row : row + 16, :])
    rows = jnp.concatenate(rows, axis=0)

    @pl.loop(0, weight.shape[1] // 256)
    def _(i):
        columns = pl.ds(pl.multiple_of(i * 256, 256), 256)
        block = dot(rows, weight[:, columns])
        for h in range(2):
            keep[h * 64 : (h + 1) * 64, columns] = block[h * 128 : h * 128 + 64]
            away[h * 64 : (h + 1) * 64, columns] = narrow(block[h * 128 + 64 : (h + 1) * 128])


def copy_kernel(piece, out):
    out[...] = piece[...]


def total_kernel(*refs):
    terms = [wide(ref[...]) for ref in refs[:-1]]
    refs[-1][...] = sum(terms[1:], terms[0])


def fold_kernel(keep, came, out):
    out[...] = (keep[...] + wide(came[...])).astype(out.dtype)


SHIFTS = (1, 3, 2, 0)
SUM_MASKS = ((4, 1, 3), (1, 4, 3), (3, 1, 4), (3, 4, 1))
GATHER_MASKS = ((4, 1, 3), (3, 4, 1), (1, 3, 4), (1, 3, 4))
ORDER = (
    "P3", "U3", "P0", "P1", "Q2", "U0", "U1", "P2", "A3", "U2", "A0", "A1",
    "B3", "B0", "A2", "B1", "S3", "S0", "S1", "J0", "B2", "J3", "J1", "K0",
    "S2", "K3", "K1", "J2", "D0", "K2", "D1", "F0", "D3", "F1", "D2", "F3",
    "F2",
)


def by_x(a):
    x = lax.axis_index("x")
    b = [a[k * 16 : (k + 1) * 16] for k in range(4)]
    odd = x % 2 == 1
    b = [jnp.where(odd, b[k ^ 1], b[k]) for k in range(4)]
    high = x // 2 == 1
    b = [jnp.where(high, b[k ^ 2], b[k]) for k in range(4)]
    return jnp.concatenate(b, axis=0)


def feed_forward(resid, normed_block, gate_weight, up_weight, down_weight):
    rows, width = normed_block.shape
    hidden_width = gate_weight.shape[1]
    z = lax.axis_index("zl")
    b16, f32 = jnp.bfloat16, jnp.float32
    normed_block = by_x(normed_block)
    near = swap(normed_block, "zh")
    pair = jnp.concatenate([jnp.where(z == 0, normed_block, near), jnp.where(z == 0, near, normed_block)], axis=0)
    pieces = [send(pair, "y", -shift) if shift % 2 else pair for shift in SHIFTS]
    state, parts = {}, {}
    last = ()

    def run(kernel, name, outs, *operands):
        nonlocal last
        outs = call(kernel, name, outs, *operands, after=last)
        last = (outs[0],)
        return outs

    def reduce(kernel, name, k, step, *operands):
        masks = SUM_MASKS[k][step:]
        part = (128 >> step, 2 * hidden_width)
        keep, away = run(functools.partial(kernel, masks), name, [(part, f32), (part, b16)], *operands)
        state[k] = [keep, exchange(away, masks[0])]

    def gather(kernel, name, k, step):
        (out,) = run(kernel, name, [((32 << step, hidden_width), b16)], *state[k])
        state[k] = [out, exchange(out, GATHER_MASKS[k][step])]

    for step in ORDER:
        kind, k = step[0], int(step[1])
        if kind == "Q":
            (piece,) = run(copy_kernel, "far", [((128, width), b16)], pair)
            pieces[k] = send(piece, "y", -SHIFTS[k])
        elif kind == "P":
            (piece,) = run(copy_kernel, "piece", [((128, width), b16)], pieces[k])
            state[k] = [piece, swap(piece, "c")]
        elif kind == "U":
            reduce(up_kernel, "up", k, 0, *state[k], gate_weight, up_weight)
        elif kind in "AB":
            reduce(add_kernel, "add", k, 1 + "AB".index(kind), *state[k])
        elif kind == "S":
            gather(hidden_kernel, "hidden", k, 0)
        elif kind in "JK":
            gather(join_kernel, "join", k, 1 + "JK".index(kind))
        elif kind == "D":
            part = (128, width)
            kernel = functools.partial(down_kernel, GATHER_MASKS[k])
            keep, away = run(kernel, "down", [(part, f32), (part, b16)], *state[k], down_weight)
            state[k] = [keep, swap(away, "c")]
        else:
            (part,) = run(fold_kernel, "fold", [((128, width), b16 if SHIFTS[k] else f32)], *state[k])
            parts[k] = send(part, "y", SHIFTS[k]) if SHIFTS[k] else part
    (total,) = run(total_kernel, "total", [((128, width), f32)], *parts.values())
    total = total.reshape(2, rows, width)
    mine = jnp.where(z == 0, total[0], total[1])
    theirs = jnp.where(z == 0, total[1], total[0])
    ffn_block = by_x(mine + wide(swap(narrow(theirs), "zh")))
    return narrow(resid + ffn_block)


def solution(mesh):
    fine = Mesh(mesh.devices.reshape(4, 2, 2, 2, 4), GX + GY)
    rows = P(GX + GY)
    return jax.shard_map(
        on_device,
        mesh=fine,
        in_specs=(rows,) * 7 + (P(), P(GY, GX), P(GY, GX), P(GX, GY)),
        out_specs=P(GX, GY),
        check_vma=False,
    )
```

```python
import functools

import jax
import jax.numpy as jnp
from jax import lax
from jax.experimental import pallas as pl
from jax.experimental.pallas import tpu as pltpu
from jax.sharding import Mesh, PartitionSpec as P

HD = 128
KVH = 8
PAGE = 16
CAP = 2
GX = ("y", "zh", "c")
GY = ("zl", "x")
CHIPS = ("y", "zh")
SWAP = [(0, 1), (1, 0)]


def attend_kernel(table, context, queries, pool, arrived, _, out, store, sems):
    row_count, blocks = table.shape
    resident = pool.shape[0]
    heads = queries.shape[1] // KVH
    span = blocks * PAGE

    @pl.loop(0, row_count)
    def _(t):
        for i in range(blocks):
            page = table[t, i]
            place = store.at[t, :, pl.ds(i * PAGE, PAGE)]

            @pl.when(page < resident)
            def _():
                pltpu.make_async_copy(pool.at[page], place, sems.at[t]).start()

            @pl.when(page >= resident)
            def _():
                pltpu.make_async_copy(arrived.at[page - resident], place, sems.at[t]).start()

    @pl.loop(0, row_count)
    def _(t):
        pltpu.make_async_copy(store.at[t], store.at[t], sems.at[t]).wait()
        scores = jnp.concatenate(
            [
                lax.dot_general(
                    queries[t, k * heads : (k + 1) * heads, :],
                    store[t, 0, :, k * HD : (k + 1) * HD],
                    (((1,), (1,)), ((), ())),
                    preferred_element_type=jnp.float32,
                )
                for k in range(KVH)
            ],
            axis=0,
        ) * (1.0 / HD**0.5)
        visible = lax.broadcasted_iota(jnp.int32, scores.shape, 1) < context[t]
        scores = jnp.where(visible, scores, jnp.float32(-1e30))
        weights = jnp.exp(scores - jnp.max(scores, axis=1, keepdims=True))
        probs = narrow(weights / jnp.sum(weights, axis=1, keepdims=True))
        for k in range(KVH):
            rows = slice(k * heads, (k + 1) * heads)
            out[t, rows, :] = dot(probs[rows], store[t, 1, :, k * HD : (k + 1) * HD])


def attend(tokens, queries, page_pool, new_pages, page_table, block_table, context, after):
    row_count, model_width = tokens.shape
    area_size = lax.axis_size(GX) * CAP
    send_slot = page_table[:, 0] * CAP + page_table[:, 1]
    holder = jnp.argmax(jnp.arange(area_size)[:, None] == send_slot[None, :], axis=1)
    arrived = lax.all_to_all(new_pages[holder], GX, split_axis=0, concat_axis=0, tiled=True)
    heads = model_width // HD
    span = block_table.shape[1] * PAGE
    smem, vmem, anywhere = (pl.BlockSpec(memory_space=m) for m in (pltpu.SMEM, pltpu.VMEM, pl.ANY))
    attended = pl.pallas_call(
        attend_kernel,
        name="attend",
        out_shape=jax.ShapeDtypeStruct((row_count, heads, HD), jnp.float32),
        in_specs=[smem, smem, vmem] + [anywhere] * 3,
        out_specs=vmem,
        scratch_shapes=[
            pltpu.VMEM((row_count, 2, span, KVH * HD), jnp.bfloat16),
            pltpu.SemaphoreType.DMA((row_count,)),
        ],
        cost_estimate=pl.CostEstimate(flops=2**27, bytes_accessed=2**23, transcendentals=2**17),
        compiler_params=pltpu.CompilerParams(vmem_limit_bytes=8 * 2**20),
    )(block_table, context, queries.reshape(row_count, heads, HD), page_pool, arrived, after)
    return narrow(wide(tokens) + attended.reshape(row_count, model_width))


def spread(mixed_rows, norm_gain):
    row_count, model_width = mixed_rows.shape
    parts = lax.axis_size(GY)
    width = model_width // parts
    mixed_wide = mixed_rows.astype(jnp.float32)
    scale = lax.rsqrt(jnp.mean(mixed_wide * mixed_wide, axis=-1, keepdims=True) + 1e-05)
    high = scale.astype(jnp.bfloat16)
    rest = scale - high.astype(jnp.float32)
    middle = rest.astype(jnp.bfloat16)
    low = (rest - middle.astype(jnp.float32)).astype(jnp.bfloat16)
    terms = jnp.concatenate([high, middle, low, jnp.zeros((row_count, 125), jnp.bfloat16)], axis=1)
    payload = jnp.concatenate(
        [
            mixed_rows.reshape(row_count, parts, width),
            jnp.broadcast_to(terms[:, None, :], (row_count, parts, 128)),
        ],
        axis=2,
    )
    near = ("zh",) + GY
    payload = jnp.concatenate([payload, payload], axis=1)
    block = lax.all_to_all(payload, near, split_axis=1, concat_axis=0, tiled=True)
    block = block.reshape(2, row_count * parts, width + 128)
    mixed = block[:, :, :width].astype(jnp.float32)
    scale = (
        block[:, :, width : width + 1].astype(jnp.float32)
        + block[:, :, width + 1 : width + 2].astype(jnp.float32)
        + block[:, :, width + 2 : width + 3].astype(jnp.float32)
    )
    gain = lax.dynamic_slice(norm_gain, (lax.axis_index(GY) * width,), (width,))
    normed = (mixed * scale * gain).astype(jnp.bfloat16)
    zh, zl = lax.axis_index("zh"), lax.axis_index("zl")
    resid = jnp.where(zh == 0, mixed[0], mixed[1])
    in_order = zh == zl
    pair = [jnp.where(in_order, normed[0], normed[1]), jnp.where(in_order, normed[1], normed[0])]
    return resid, jnp.concatenate([by_x(half) for half in pair], axis=0)


def on_device(
    tokens,
    queries,
    page_pool,
    new_pages,
    page_table,
    block_table,
    context,
    norm_gain,
    gate_weight,
    up_weight,
    down_weight,
):
    gate_weight, up_weight, down_weight, mark = load(gate_weight, up_weight, down_weight)
    mixed_rows = attend(tokens, queries, page_pool, new_pages, page_table, block_table, context, mark)
    resid, pair = spread(mixed_rows, norm_gain)

    return feed_forward(resid, pair, gate_weight, up_weight, down_weight)


def dot(a, b):
    return jnp.dot(a, b, preferred_element_type=jnp.float32)


def wide(a):
    return a.astype(jnp.float32)


def narrow(a):
    return a.astype(jnp.bfloat16)


def swap(a, axis):
    return lax.ppermute(a, axis, [(0, 1), (1, 0)])


def send(a, axis, shift):
    return lax.ppermute(a, axis, [(i, (i + shift) % 4) for i in range(4)])


def home(a, shift, cross):
    pairs = [(y * 2 + h, (y + shift) % 4 * 2 + (h ^ cross)) for y in range(4) for h in range(2)]
    return lax.ppermute(a, CHIPS, pairs)


def call(kernel, name, outs, *operands, after=()):
    count = len(operands)
    vmem, anywhere = pl.BlockSpec(memory_space=pltpu.VMEM), pl.BlockSpec(memory_space=pl.ANY)
    return pl.pallas_call(
        lambda *refs: kernel(*refs[:count], *refs[count + len(after) :]),
        name=name,
        out_shape=[jax.ShapeDtypeStruct(shape, dtype) for shape, dtype in outs],
        in_specs=[vmem] * count + [anywhere] * len(after),
        out_specs=[vmem] * len(outs),
        cost_estimate=pl.CostEstimate(flops=2**34, bytes_accessed=1024, transcendentals=0),
        compiler_params=pltpu.CompilerParams(vmem_limit_bytes=8 * 2**20),
    )(*operands, *after)


def load_kernel(*refs):
    mark, sems = refs[-2:]
    count = len(refs) // 2 - 1
    mark[...] = jnp.zeros_like(mark)
    copies = [pltpu.make_async_copy(refs[i], refs[count + i], sems.at[i]) for i in range(count)]
    for copy in copies:
        copy.start()
    for copy in copies:
        copy.wait()


def load(*weights):
    return pl.pallas_call(
        load_kernel,
        name="load",
        out_shape=[pltpu.VMEM(w.shape, w.dtype) for w in weights] + [jax.ShapeDtypeStruct((8, 128), jnp.float32)],
        in_specs=[pl.BlockSpec(memory_space=pltpu.HBM)] * len(weights),
        out_specs=[pl.BlockSpec(memory_space=pltpu.VMEM)] * (len(weights) + 1),
        scratch_shapes=[pltpu.SemaphoreType.DMA((len(weights),))],
        cost_estimate=pl.CostEstimate(flops=0, bytes_accessed=2**25, transcendentals=0),
        compiler_params=pltpu.CompilerParams(vmem_limit_bytes=8 * 2**20),
    )(*weights)


def span(masks):
    names = [0]
    for mask in masks:
        names = names + [name ^ mask for name in names]
    return names


def exchange(a, mask):
    if mask == 4:
        return lax.ppermute(a, "zl", [(0, 1), (1, 0)])
    return lax.ppermute(a, "x", [(i, i ^ mask) for i in range(4)])


def up_kernel(masks, own, other, gate, up, keep, away):
    width = gate.shape[1]
    whole = width // 256 * 256
    kept = span(masks[1:])

    def put(columns, block):
        for h in range(2):
            for j in range(2):
                for d in range(4):
                    name, row = h * 4 + d, ((h * 2 + j) * 4 + d) * 16
                    out = keep if name in kept else away
                    place = kept.index(name if name in kept else name ^ masks[0]) * 32 + j * 16
                    out[place : place + 16, columns] = block[row : row + 16].astype(out.dtype)

    rows = jnp.concatenate([core[h * 64 : (h + 1) * 64, :] for h in range(2) for core in (own, other)], axis=0)

    @pl.loop(0, whole // 256)
    def _(i):
        start = pl.multiple_of(i * 256, 256)
        put(pl.ds(start, 256), dot(rows, gate[:, pl.ds(start, 256)]))
        put(pl.ds(pl.multiple_of(width + start, 128), 256), dot(rows, up[:, pl.ds(start, 256)]))

    last = dot(rows, jnp.concatenate([gate[:, whole:], up[:, whole:]], axis=1))
    put(pl.ds(whole, width - whole), last[:, : width - whole])
    put(pl.ds(width + whole, width - whole), last[:, width - whole :])


def add_kernel(masks, mine, came, keep, away):
    names, kept = span(masks), span(masks[1:])
    for out, flip in ((keep, 0), (away, masks[0])):
        for place, name in enumerate(kept):
            row = names.index(name ^ flip) * 32
            total = mine[row : row + 32, :] + wide(came[row : row + 32, :])
            out[place * 32 : (place + 1) * 32, :] = total.astype(out.dtype)


def hidden_kernel(mine, came, out):
    width = out.shape[1]

    def total(columns):
        return mine[:, columns] + wide(came[:, columns])

    gate = total(slice(0, width))
    out[...] = narrow(gate * (1.0 / (1.0 + jnp.exp(-gate))) * total(slice(width, 2 * width)))


def join_kernel(mine, came, out):
    rows = mine.shape[0]
    out[:rows, :] = mine[...]
    out[rows:, :] = came[...]


def down_kernel(masks, mine, came, weight, keep, away):
    names, rows = span(masks), []
    for h in range(2):
        for j in range(2):
            for d in range(4):
                half, place = divmod(names.index(h * 4 + d), 4)
                row = place * 32 + j * 16
                rows.append((mine, came)[half][row : row + 16, :])
    rows = jnp.concatenate(rows, axis=0)

    @pl.loop(0, weight.shape[1] // 256)
    def _(i):
        columns = pl.ds(pl.multiple_of(i * 256, 256), 256)
        block = dot(rows, weight[:, columns])
        for h in range(2):
            keep[h * 64 : (h + 1) * 64, columns] = block[h * 128 : h * 128 + 64]
            away[h * 64 : (h + 1) * 64, columns] = narrow(block[h * 128 + 64 : (h + 1) * 128])


def copy_kernel(piece, out):
    out[...] = piece[...]


def total_kernel(*refs):
    terms = [wide(ref[...]) for ref in refs[:-1]]
    refs[-1][...] = sum(terms[1:], terms[0])


def fold_kernel(keep, came, out):
    out[...] = (keep[...] + wide(came[...])).astype(out.dtype)


SHIFTS = (1, 3, 2, 0)
SUM_MASKS = ((3, 1, 4), (1, 4, 3), (3, 4, 1), (1, 4, 3))
GATHER_MASKS = ((3, 4, 1), (1, 4, 3), (3, 4, 1), (4, 3, 1))
ORDER = (
    "P3", "U3", "Q2", "P0", "P1", "U0", "U1", "P2", "A3", "U2", "A0", "B3",
    "A1", "B0", "A2", "B1", "S3", "S0", "S1", "J0", "B2", "J3", "J1", "K0",
    "S2", "K3", "K1", "J2", "D0", "K2", "D1", "F0", "D3", "F1", "D2", "F3",
    "F2",
)


def by_x(a):
    x = lax.axis_index("x")
    b = [a[k * 16 : (k + 1) * 16] for k in range(4)]
    odd = x % 2 == 1
    b = [jnp.where(odd, b[k ^ 1], b[k]) for k in range(4)]
    high = x // 2 == 1
    b = [jnp.where(high, b[k ^ 2], b[k]) for k in range(4)]
    return jnp.concatenate(b, axis=0)


def feed_forward(resid, pair, gate_weight, up_weight, down_weight):
    rows, width = resid.shape
    hidden_width = gate_weight.shape[1]
    z = lax.axis_index("zl")
    b16, f32 = jnp.bfloat16, jnp.float32
    pieces = [send(pair, "y", -shift) if shift % 2 else pair for shift in SHIFTS]
    state, parts = {}, []
    last = ()

    def run(kernel, name, outs, *operands):
        nonlocal last
        outs = call(kernel, name, outs, *operands, after=last)
        last = (outs[0],)
        return outs

    def reduce(kernel, name, k, step, *operands):
        masks = SUM_MASKS[k][step:]
        part = (128 >> step, 2 * hidden_width)
        keep, away = run(functools.partial(kernel, masks), name, [(part, f32), (part, b16)], *operands)
        state[k] = [keep, exchange(away, masks[0])]

    def gather(kernel, name, k, step):
        (out,) = run(kernel, name, [((32 << step, hidden_width), b16)], *state[k])
        state[k] = [out, exchange(out, GATHER_MASKS[k][step])]

    for step in ORDER:
        kind, k = step[0], int(step[1])
        if kind == "Q":
            (piece,) = run(copy_kernel, "far", [((128, width), b16)], pair)
            pieces[k] = send(piece, "y", -SHIFTS[k])
        elif kind == "P":
            (piece,) = run(copy_kernel, "piece", [((128, width), b16)], pieces[k])
            state[k] = [piece, swap(piece, "c")]
        elif kind == "U":
            reduce(up_kernel, "up", k, 0, *state[k], gate_weight, up_weight)
        elif kind in "AB":
            reduce(add_kernel, "add", k, 1 + "AB".index(kind), *state[k])
        elif kind == "S":
            gather(hidden_kernel, "hidden", k, 0)
        elif kind in "JK":
            gather(join_kernel, "join", k, 1 + "JK".index(kind))
        elif kind == "D":
            part = (128, width)
            kernel = functools.partial(down_kernel, GATHER_MASKS[k])
            keep, away = run(kernel, "down", [(part, f32), (part, b16)], *state[k], down_weight)
            state[k] = [keep, swap(away, "c")]
        else:
            (part,) = run(fold_kernel, "fold", [((128, width), f32)], *state[k])
            mine = jnp.where(z == 0, part[:rows], part[rows:])
            theirs = narrow(jnp.where(z == 0, part[rows:], part[:rows]))
            parts.append(home(theirs, SHIFTS[k], 1))
            parts.append(home(narrow(mine), SHIFTS[k], 0) if SHIFTS[k] else mine)
    (total,) = run(total_kernel, "total", [((rows, width), f32)], *parts)
    return narrow(resid + by_x(total))


def solution(mesh):
    fine = Mesh(mesh.devices.reshape(4, 2, 2, 2, 4), GX + GY)
    rows = P(GX + GY)
    return jax.shard_map(
        on_device,
        mesh=fine,
        in_specs=(rows,) * 7 + (P(), P(GY, GX), P(GY, GX), P(GX, GY)),
        out_specs=P(GX, GY),
        check_vma=False,
    )
```

```python
import functools

import jax
import jax.numpy as jnp
from jax import lax
from jax.experimental import pallas as pl
from jax.experimental.pallas import tpu as pltpu
from jax.sharding import Mesh, PartitionSpec as P

HD = 128
KVH = 8
PAGE = 16
CAP = 2
GX = ("y", "zh", "c")
GY = ("zl", "x")
CHIPS = ("y", "zh")
SWAP = [(0, 1), (1, 0)]


def attend_kernel(table, context, queries, pool, arrived, _, out, store, sems):
    row_count, blocks = table.shape
    resident = pool.shape[0]
    heads = queries.shape[1] // KVH
    span = blocks * PAGE

    @pl.loop(0, row_count)
    def _(t):
        for i in range(blocks):
            page = table[t, i]
            place = store.at[t, :, pl.ds(i * PAGE, PAGE)]

            @pl.when(page < resident)
            def _():
                pltpu.make_async_copy(pool.at[page], place, sems.at[t]).start()

            @pl.when(page >= resident)
            def _():
                pltpu.make_async_copy(arrived.at[page - resident], place, sems.at[t]).start()

    def attend_row(t):
        scores = jnp.concatenate(
            [
                lax.dot_general(
                    queries[t, k * heads : (k + 1) * heads, :],
                    store[t, 0, :, k * HD : (k + 1) * HD],
                    (((1,), (1,)), ((), ())),
                    preferred_element_type=jnp.float32,
                )
                for k in range(KVH)
            ],
            axis=0,
        ) * (1.0 / HD**0.5)
        visible = lax.broadcasted_iota(jnp.int32, scores.shape, 1) < context[t]
        scores = jnp.where(visible, scores, jnp.float32(-1e30))
        weights = jnp.exp(scores - jnp.max(scores, axis=1, keepdims=True))
        probs = narrow(weights / jnp.sum(weights, axis=1, keepdims=True))
        for k in range(KVH):
            rows = slice(k * heads, (k + 1) * heads)
            out[t, rows, :] = dot(probs[rows], store[t, 1, :, k * HD : (k + 1) * HD])

    @pl.loop(0, row_count // 4)
    def _(i):
        for t in range(4):
            pltpu.make_async_copy(store.at[i * 4 + t], store.at[i * 4 + t], sems.at[i * 4 + t]).wait()
        for t in range(4):
            attend_row(i * 4 + t)


def attend(tokens, queries, page_pool, new_pages, page_table, block_table, context, after):
    row_count, model_width = tokens.shape
    area_size = lax.axis_size(GX) * CAP
    send_slot = page_table[:, 0] * CAP + page_table[:, 1]
    holder = jnp.argmax(jnp.arange(area_size)[:, None] == send_slot[None, :], axis=1)
    arrived = lax.all_to_all(new_pages[holder], GX, split_axis=0, concat_axis=0, tiled=True)
    heads = model_width // HD
    span = block_table.shape[1] * PAGE
    smem, vmem, anywhere = (pl.BlockSpec(memory_space=m) for m in (pltpu.SMEM, pltpu.VMEM, pl.ANY))
    attended = pl.pallas_call(
        attend_kernel,
        name="attend",
        out_shape=jax.ShapeDtypeStruct((row_count, heads, HD), jnp.float32),
        in_specs=[smem, smem, vmem] + [anywhere] * 3,
        out_specs=vmem,
        scratch_shapes=[
            pltpu.VMEM((row_count, 2, span, KVH * HD), jnp.bfloat16),
            pltpu.SemaphoreType.DMA((row_count,)),
        ],
        cost_estimate=pl.CostEstimate(flops=2**27, bytes_accessed=2**23, transcendentals=2**17),
        compiler_params=pltpu.CompilerParams(vmem_limit_bytes=8 * 2**20),
    )(block_table, context, queries.reshape(row_count, heads, HD), page_pool, arrived, after)
    return narrow(wide(tokens) + attended.reshape(row_count, model_width))


def spread(mixed_rows, norm_gain):
    row_count, model_width = mixed_rows.shape
    parts = lax.axis_size(GY)
    width = model_width // parts
    mixed_wide = mixed_rows.astype(jnp.float32)
    scale = lax.rsqrt(jnp.mean(mixed_wide * mixed_wide, axis=-1, keepdims=True) + 1e-05)
    high = scale.astype(jnp.bfloat16)
    rest = scale - high.astype(jnp.float32)
    middle = rest.astype(jnp.bfloat16)
    low = (rest - middle.astype(jnp.float32)).astype(jnp.bfloat16)
    terms = jnp.concatenate([high, middle, low, jnp.zeros((row_count, 125), jnp.bfloat16)], axis=1)
    payload = jnp.concatenate(
        [
            mixed_rows.reshape(row_count, parts, width),
            jnp.broadcast_to(terms[:, None, :], (row_count, parts, 128)),
        ],
        axis=2,
    )
    near = ("zh",) + GY
    payload = jnp.concatenate([payload, payload], axis=1)
    block = lax.all_to_all(payload, near, split_axis=1, concat_axis=0, tiled=True)
    block = block.reshape(2, row_count * parts, width + 128)
    mixed = block[:, :, :width].astype(jnp.float32)
    scale = (
        block[:, :, width : width + 1].astype(jnp.float32)
        + block[:, :, width + 1 : width + 2].astype(jnp.float32)
        + block[:, :, width + 2 : width + 3].astype(jnp.float32)
    )
    gain = lax.dynamic_slice(norm_gain, (lax.axis_index(GY) * width,), (width,))
    normed = (mixed * scale * gain).astype(jnp.bfloat16)
    zh, zl = lax.axis_index("zh"), lax.axis_index("zl")
    resid = jnp.where(zh == 0, mixed[0], mixed[1])
    in_order = zh == zl
    pair = [jnp.where(in_order, normed[0], normed[1]), jnp.where(in_order, normed[1], normed[0])]
    return resid, jnp.concatenate([by_x(half) for half in pair], axis=0)


def on_device(
    tokens,
    queries,
    page_pool,
    new_pages,
    page_table,
    block_table,
    context,
    norm_gain,
    gate_weight,
    up_weight,
    down_weight,
):
    gate_weight, up_weight, down_weight, mark = load(gate_weight, up_weight, down_weight)
    mixed_rows = attend(tokens, queries, page_pool, new_pages, page_table, block_table, context, mark)
    resid, pair = spread(mixed_rows, norm_gain)

    return feed_forward(resid, pair, gate_weight, up_weight, down_weight)


def dot(a, b):
    return jnp.dot(a, b, preferred_element_type=jnp.float32)


def wide(a):
    return a.astype(jnp.float32)


def narrow(a):
    return a.astype(jnp.bfloat16)


def swap(a, axis):
    return lax.ppermute(a, axis, [(0, 1), (1, 0)])


def send(a, axis, shift):
    return lax.ppermute(a, axis, [(i, (i + shift) % 4) for i in range(4)])


def home(a, shift, cross):
    pairs = [(y * 2 + h, (y + shift) % 4 * 2 + (h ^ cross)) for y in range(4) for h in range(2)]
    return lax.ppermute(a, CHIPS, pairs)


def call(kernel, name, outs, *operands, after=()):
    count = len(operands)
    vmem, anywhere = pl.BlockSpec(memory_space=pltpu.VMEM), pl.BlockSpec(memory_space=pl.ANY)
    return pl.pallas_call(
        lambda *refs: kernel(*refs[:count], *refs[count + len(after) :]),
        name=name,
        out_shape=[jax.ShapeDtypeStruct(shape, dtype) for shape, dtype in outs],
        in_specs=[vmem] * count + [anywhere] * len(after),
        out_specs=[vmem] * len(outs),
        cost_estimate=pl.CostEstimate(flops=2**34, bytes_accessed=1024, transcendentals=0),
        compiler_params=pltpu.CompilerParams(vmem_limit_bytes=8 * 2**20),
    )(*operands, *after)


def load_kernel(*refs):
    mark, sems = refs[-2:]
    count = len(refs) // 2 - 1
    mark[...] = jnp.zeros_like(mark)
    copies = [pltpu.make_async_copy(refs[i], refs[count + i], sems.at[i]) for i in range(count)]
    for copy in copies:
        copy.start()
    for copy in copies:
        copy.wait()


def load(*weights):
    return pl.pallas_call(
        load_kernel,
        name="load",
        out_shape=[pltpu.VMEM(w.shape, w.dtype) for w in weights] + [jax.ShapeDtypeStruct((8, 128), jnp.float32)],
        in_specs=[pl.BlockSpec(memory_space=pltpu.HBM)] * len(weights),
        out_specs=[pl.BlockSpec(memory_space=pltpu.VMEM)] * (len(weights) + 1),
        scratch_shapes=[pltpu.SemaphoreType.DMA((len(weights),))],
        cost_estimate=pl.CostEstimate(flops=0, bytes_accessed=2**25, transcendentals=0),
        compiler_params=pltpu.CompilerParams(vmem_limit_bytes=8 * 2**20),
    )(*weights)


def span(masks):
    names = [0]
    for mask in masks:
        names = names + [name ^ mask for name in names]
    return names


def exchange(a, mask):
    if mask == 4:
        return lax.ppermute(a, "zl", [(0, 1), (1, 0)])
    return lax.ppermute(a, "x", [(i, i ^ mask) for i in range(4)])


def up_kernel(masks, own, other, gate, up, keep, away):
    width = gate.shape[1]
    whole = width // 256 * 256
    kept = span(masks[1:])

    def put(columns, block):
        for h in range(2):
            for j in range(2):
                for d in range(4):
                    name, row = h * 4 + d, ((h * 2 + j) * 4 + d) * 16
                    out = keep if name in kept else away
                    place = kept.index(name if name in kept else name ^ masks[0]) * 32 + j * 16
                    out[place : place + 16, columns] = block[row : row + 16].astype(out.dtype)

    rows = jnp.concatenate([core[h * 64 : (h + 1) * 64, :] for h in range(2) for core in (own, other)], axis=0)

    @pl.loop(0, whole // 256)
    def _(i):
        start = pl.multiple_of(i * 256, 256)
        put(pl.ds(start, 256), dot(rows, gate[:, pl.ds(start, 256)]))
        put(pl.ds(pl.multiple_of(width + start, 128), 256), dot(rows, up[:, pl.ds(start, 256)]))

    last = dot(rows, jnp.concatenate([gate[:, whole:], up[:, whole:]], axis=1))
    put(pl.ds(whole, width - whole), last[:, : width - whole])
    put(pl.ds(width + whole, width - whole), last[:, width - whole :])


def add_kernel(masks, mine, came, keep, away):
    names, kept = span(masks), span(masks[1:])
    for out, flip in ((keep, 0), (away, masks[0])):
        for place, name in enumerate(kept):
            row = names.index(name ^ flip) * 32
            total = mine[row : row + 32, :] + wide(came[row : row + 32, :])
            out[place * 32 : (place + 1) * 32, :] = total.astype(out.dtype)


def hidden_kernel(mine, came, out):
    width = out.shape[1]

    def total(columns):
        return mine[:, columns] + wide(came[:, columns])

    gate = total(slice(0, width))
    out[...] = narrow(gate * (1.0 / (1.0 + jnp.exp(-gate))) * total(slice(width, 2 * width)))


def join_kernel(mine, came, out):
    rows = mine.shape[0]
    out[:rows, :] = mine[...]
    out[rows:, :] = came[...]


def down_kernel(masks, mine, came, weight, keep, away):
    names, rows = span(masks), []
    for h in range(2):
        for j in range(2):
            for d in range(4):
                half, place = divmod(names.index(h * 4 + d), 4)
                row = place * 32 + j * 16
                rows.append((mine, came)[half][row : row + 16, :])
    rows = jnp.concatenate(rows, axis=0)

    @pl.loop(0, weight.shape[1] // 256)
    def _(i):
        columns = pl.ds(pl.multiple_of(i * 256, 256), 256)
        block = dot(rows, weight[:, columns])
        for h in range(2):
            keep[h * 64 : (h + 1) * 64, columns] = block[h * 128 : h * 128 + 64]
            away[h * 64 : (h + 1) * 64, columns] = narrow(block[h * 128 + 64 : (h + 1) * 128])


def copy_kernel(piece, out):
    out[...] = piece[...]


def total_kernel(*refs):
    terms = [wide(ref[...]) for ref in refs[:-1]]
    refs[-1][...] = sum(terms[1:], terms[0])


def fold_kernel(keep, came, out):
    out[...] = (keep[...] + wide(came[...])).astype(out.dtype)


SHIFTS = (1, 3, 2, 0)
SUM_MASKS = ((3, 1, 4), (1, 4, 3), (3, 4, 1), (1, 4, 3))
GATHER_MASKS = ((3, 4, 1), (1, 4, 3), (3, 4, 1), (4, 3, 1))
ORDER = (
    "P3", "U3", "Q2", "P0", "P1", "U0", "U1", "P2", "A3", "U2", "A0", "B3",
    "A1", "B0", "A2", "B1", "S3", "S0", "S1", "J0", "B2", "J3", "J1", "K0",
    "S2", "K3", "K1", "J2", "D0", "K2", "D1", "F0", "D3", "F1", "D2", "F3",
    "F2",
)


def by_x(a):
    x = lax.axis_index("x")
    b = [a[k * 16 : (k + 1) * 16] for k in range(4)]
    odd = x % 2 == 1
    b = [jnp.where(odd, b[k ^ 1], b[k]) for k in range(4)]
    high = x // 2 == 1
    b = [jnp.where(high, b[k ^ 2], b[k]) for k in range(4)]
    return jnp.concatenate(b, axis=0)


def feed_forward(resid, pair, gate_weight, up_weight, down_weight):
    rows, width = resid.shape
    hidden_width = gate_weight.shape[1]
    z = lax.axis_index("zl")
    b16, f32 = jnp.bfloat16, jnp.float32
    pieces = [send(pair, "y", -shift) if shift % 2 else pair for shift in SHIFTS]
    state, parts = {}, []
    last = ()

    def run(kernel, name, outs, *operands):
        nonlocal last
        outs = call(kernel, name, outs, *operands, after=last)
        last = (outs[0],)
        return outs

    def reduce(kernel, name, k, step, *operands):
        masks = SUM_MASKS[k][step:]
        part = (128 >> step, 2 * hidden_width)
        keep, away = run(functools.partial(kernel, masks), name, [(part, f32), (part, b16)], *operands)
        state[k] = [keep, exchange(away, masks[0])]

    def gather(kernel, name, k, step):
        (out,) = run(kernel, name, [((32 << step, hidden_width), b16)], *state[k])
        state[k] = [out, exchange(out, GATHER_MASKS[k][step])]

    for step in ORDER:
        kind, k = step[0], int(step[1])
        if kind == "Q":
            (piece,) = run(copy_kernel, "far", [((128, width), b16)], pair)
            pieces[k] = send(piece, "y", -SHIFTS[k])
        elif kind == "P":
            (piece,) = run(copy_kernel, "piece", [((128, width), b16)], pieces[k])
            state[k] = [piece, swap(piece, "c")]
        elif kind == "U":
            reduce(up_kernel, "up", k, 0, *state[k], gate_weight, up_weight)
        elif kind in "AB":
            reduce(add_kernel, "add", k, 1 + "AB".index(kind), *state[k])
        elif kind == "S":
            gather(hidden_kernel, "hidden", k, 0)
        elif kind in "JK":
            gather(join_kernel, "join", k, 1 + "JK".index(kind))
        elif kind == "D":
            part = (128, width)
            kernel = functools.partial(down_kernel, GATHER_MASKS[k])
            keep, away = run(kernel, "down", [(part, f32), (part, b16)], *state[k], down_weight)
            state[k] = [keep, swap(away, "c")]
        else:
            (part,) = run(fold_kernel, "fold", [((128, width), f32)], *state[k])
            mine = jnp.where(z == 0, part[:rows], part[rows:])
            theirs = narrow(jnp.where(z == 0, part[rows:], part[:rows]))
            parts.append(home(theirs, SHIFTS[k], 1))
            parts.append(home(narrow(mine), SHIFTS[k], 0) if SHIFTS[k] else mine)
    (total,) = run(total_kernel, "total", [((rows, width), f32)], *parts)
    return narrow(resid + by_x(total))


def solution(mesh):
    fine = Mesh(mesh.devices.reshape(4, 2, 2, 2, 4), GX + GY)
    rows = P(GX + GY)
    return jax.shard_map(
        on_device,
        mesh=fine,
        in_specs=(rows,) * 7 + (P(), P(GY, GX), P(GY, GX), P(GX, GY)),
        out_specs=P(GX, GY),
        check_vma=False,
    )
```
